32 devices in a mesh: tm: 8 (over y, x, core), col: 4 (over z).
Axes of the slice: x: 2, y: 2, z: 4, core: 2. Of those that a mesh axis runs over, the one named last changes fastest.
Arguments:
- panel: bfloat16 [1024, 131072], P('col', 'tm'), may hold values from -60 to 60
- response: float32 [131072], replicated, may hold values from 0.25 to 2.5
Outputs:
- normal: float32 [1024, 1024], P('col', 'tm')
The draws below stay inside these ranges and needn't reach their ends.
All inputs are finite; a program needn't handle non-finite values.
Results may differ from the reference program's by a relative error of at most 0.0015.
Values may be sent and summed in bfloat16 or wider, within the bound.
A program may use at most 192 MiB of HBM per device.

```python
import math
import jax
import jax.numpy as jnp
from jax import lax

COLS = 1024
EPOCHS = 131072


def draw_panel(key, part):
    key_list = jax.random.split(jax.random.fold_in(key, 7001), 6)
    noise_part = jax.random.truncated_normal(key_list[0], -4.0, 4.0, (COLS, EPOCHS), jnp.float32)
    level_log = jax.random.uniform(key_list[1], (COLS, 64), jnp.float32, math.log(0.3), math.log(3.0))
    levels = jnp.repeat(jnp.exp(level_log), EPOCHS // 64, axis=1)
    tone_freq = jax.random.randint(key_list[2], (16, 1), 1, EPOCHS // 2, jnp.int32)
    epoch_index = jnp.arange(EPOCHS, dtype=jnp.int32)[None, :]
    upper_part = tone_freq * (epoch_index // 256) % EPOCHS
    phase_index = (upper_part * 256 + tone_freq * (epoch_index % 256)) % EPOCHS
    tone_angle = phase_index.astype(jnp.float32) * (2.0 * math.pi / EPOCHS)
    envelope_log = jax.random.uniform(key_list[3], (16, 64), jnp.float32, math.log(0.5), math.log(2.0))
    envelope = jnp.repeat(jnp.exp(envelope_log), EPOCHS // 64, axis=1)
    basis_cos = jnp.cos(tone_angle) * envelope
    basis_sin = jnp.sin(tone_angle) * envelope
    amplitude = 0.35 * jax.random.truncated_normal(key_list[4], -4.0, 4.0, (COLS, 16), jnp.float32)
    offset = jax.random.uniform(key_list[5], (COLS, 16), jnp.float32, -math.pi, math.pi)
    tone_part = jnp.dot(amplitude * jnp.cos(offset), basis_cos, precision=lax.Precision.HIGHEST)
    tone_part = tone_part - jnp.dot(amplitude * jnp.sin(offset), basis_sin, precision=lax.Precision.HIGHEST)
    return (noise_part * levels + tone_part).astype(jnp.bfloat16)


def setup_inputs(seed: int = 0) -> dict:
    seeds = jax.random.split(jax.random.key(seed), 3)
    panel = draw_panel(jax.random.fold_in(seeds[2], 71), 0)
    response = jnp.clip(jnp.exp(jax.random.uniform(seeds[1], (EPOCHS,), jnp.float32, math.log(0.25), math.log(2.5))), 0.25, 2.5)
    return {"panel": panel, "response": response}


def whiten_block(panel_block, response):
    spectrum = jnp.fft.fft(panel_block.astype(jnp.float32), axis=1)
    filtered = jnp.fft.ifft(spectrum * response, axis=1)
    return jnp.real(filtered).astype(jnp.bfloat16)


def reference(panel, response):
    panel_blocks = panel.reshape(COLS // 64, 64, EPOCHS)
    whitened = lax.map(lambda block_rows: whiten_block(block_rows, response), panel_blocks)
    whitened = whitened.reshape(COLS, EPOCHS)
    normal = lax.dot_general(whitened, whitened, (((1,), (1,)), ((), ())), preferred_element_type=jnp.float32)
    return normal / EPOCHS
```

```python
import functools
import math

import jax
import jax.numpy as jnp
import numpy as np
from jax import lax
from jax.experimental import pallas as pl
from jax.experimental.pallas import tpu as pltpu
from jax.sharding import PartitionSpec as P

INNER = 256
LANES = 128
VMEM_BYTES = 58 * 1024 * 1024


def split_table(table):
    upper = np.asarray(table, np.float32).astype(jnp.bfloat16)
    lower = (np.asarray(table, np.float64) - upper.astype(np.float64)).astype(jnp.bfloat16)
    return np.stack([upper, lower])


def make_tables(total_len):
    outer = total_len // INNER
    half = outer // 2
    row = np.arange(half)[:, None]
    angle = 2.0 * math.pi * (row * np.arange(outer)[None, :] % outer) / outer
    cosine, sine = np.cos(angle), -np.sin(angle)
    sine[0] = 1.0 - 2.0 * (np.arange(outer) % 2)
    first = split_table(np.concatenate([cosine, sine]))
    lane = np.arange(INNER)
    angle = 2.0 * math.pi * (row * lane[None, :] % total_len) / total_len
    twist = np.stack([np.cos(angle), np.sin(angle)]).astype(np.float32)
    angle = 2.0 * math.pi * (lane[:, None] * lane[None, :] % INNER) / INNER
    cosine, sine = np.cos(angle), np.sin(angle)
    inner = split_table(np.block([[cosine, -sine], [sine, cosine]]))
    back = split_table(np.block([[cosine, sine], [-sine, cosine]]))
    return first, twist, inner, back


def gain_tables(response, total_len):
    outer = total_len // INNER
    half = outer // 2
    mirrored = jnp.concatenate([response[:1], jnp.flip(response[1:])])
    gain = 0.5 * (response + mirrored)
    grid = gain.reshape(INNER, outer).T
    wide = jnp.tile(grid[:half] * (math.sqrt(2.0) / INNER), (1, 2))
    lane = np.arange(INNER)
    blocks = []
    for shift, channel in ((0, 0), (1, half)):
        angle = math.pi * (lane[:, None] * (2 * lane[None, :] + shift) % (2 * INNER)) / INNER
        basis = np.concatenate([np.cos(angle), np.sin(angle)], axis=1).astype(np.float32)
        scaled = basis * jnp.tile(grid[channel] / INNER, 2)[None, :]
        blocks.append(jnp.dot(scaled, basis.T, precision=lax.Precision.HIGHEST))
    zero = jnp.zeros_like(blocks[0])
    edge = jnp.concatenate(
        [jnp.concatenate([blocks[0], zero], axis=1), jnp.concatenate([zero, blocks[1]], axis=1)]
    )
    upper = edge.astype(jnp.bfloat16)
    lower = (edge - upper.astype(jnp.float32)).astype(jnp.bfloat16)
    return wide, jnp.stack([upper, lower])


def product(left, right):
    return jnp.dot(left, right, preferred_element_type=jnp.float32)


def outer_stage(values, first, twist, mixed, index, count):
    half = twist.shape[1]
    sums = product(first[0], values) + product(first[1], values)
    real, imag = sums[:half], sums[half:]
    cosine, sine = twist[0], twist[1]
    turned = (real * cosine + imag * sine, imag * cosine - real * sine)
    for piece in range(2 * INNER // LANES):
        part, lane = divmod(piece * LANES, INNER)
        mixed.at[piece][pl.ds(index, half, stride=count), :] = turned[part][:, lane : lane + LANES]


def mixed_rows(mixed, start, size):
    return jnp.concatenate([mixed[piece, pl.ds(start, size), :] for piece in range(mixed.shape[0])], axis=1)


def inner_stage(values, gain, inner, back):
    rows = values.astype(jnp.bfloat16)
    spectrum = product(rows, inner[0]) + product(rows, inner[1])
    channels = gain.shape[0]
    spectrum = spectrum.reshape(channels, -1, 2 * INNER) * gain[:, None, :]
    spectrum = spectrum.reshape(-1, 2 * INNER)
    upper = spectrum.astype(jnp.bfloat16)
    lower = (spectrum - upper.astype(jnp.float32)).astype(jnp.bfloat16)
    return product(upper, back[0]) + product(lower, back[0]) + product(upper, back[1])


def edge_stage(values, edge):
    rows = values.astype(jnp.bfloat16)
    return product(rows, edge[0]) + product(rows, edge[1])


def filter_kernel(panel_ref, first_ref, twist_ref, inner_ref, back_ref, gain_ref, edge_ref, out_ref, mixed):
    sources, count, steps, _ = panel_ref.shape
    half = twist_ref.shape[1]

    @pl.loop(0, count)
    def _(index):
        values = panel_ref[:, index].reshape(sources * steps, INNER)
        outer_stage(values, first_ref, twist_ref, mixed, index, count)

    channels = min(half, 32)

    @pl.loop(0, half // channels)
    def _(tile):
        start = pl.multiple_of(tile * channels, channels)
        rows = mixed_rows(mixed, start * count, channels * count)
        result = inner_stage(rows, gain_ref[pl.ds(start, channels), :], inner_ref, back_ref)
        out_ref[pl.ds(start, channels)] = result.reshape(channels, count, 2 * INNER).astype(out_ref.dtype)

    out_ref[0] = edge_stage(mixed_rows(mixed, 0, count), edge_ref).astype(out_ref.dtype)


def filter_columns(series, tables, gains):
    first, twist, inner, back = tables
    gain, edge = gains
    sources, columns, steps, _ = series.shape
    half = twist.shape[1]
    count = math.gcd(columns, 16)
    whole = lambda array: pl.BlockSpec(array.shape, lambda step: (0,) * array.ndim)
    return pl.pallas_call(
        filter_kernel,
        grid=(columns // count,),
        in_specs=[
            pl.BlockSpec((sources, count, steps, INNER), lambda step: (0, step, 0, 0)),
            *map(whole, (first, twist, inner, back, gain, edge)),
        ],
        out_specs=pl.BlockSpec((half, count, 2 * INNER), lambda step: (0, step, 0)),
        out_shape=jax.ShapeDtypeStruct((half, columns, 2 * INNER), jnp.bfloat16),
        scratch_shapes=[pltpu.VMEM((2 * INNER // LANES, half * count, LANES), jnp.float32)],
        compiler_params=pltpu.CompilerParams(vmem_limit_bytes=VMEM_BYTES),
    )(series, first, twist, inner, back, gain, edge)


def gram_kernel(left_ref, right_ref, out_ref, *, scale):
    step = pl.program_id(2)

    @pl.when(step == 0)
    def _():
        out_ref[...] = jnp.zeros_like(out_ref)

    out_ref[...] += lax.dot_general(
        left_ref[0], right_ref[0], (((1,), (1,)), ((), ())), preferred_element_type=jnp.float32
    )

    @pl.when(step == pl.num_programs(2) - 1)
    def _():
        out_ref[...] = out_ref[...] * scale


def gram(values, scale):
    channels, columns, depth = values.shape
    block = math.gcd(columns, 512)
    return pl.pallas_call(
        functools.partial(gram_kernel, scale=scale),
        grid=(columns // block, columns // block, channels),
        in_specs=[
            pl.BlockSpec((1, block, depth), lambda i, j, k: (k, i, 0)),
            pl.BlockSpec((1, block, depth), lambda i, j, k: (k, j, 0)),
        ],
        out_specs=pl.BlockSpec((block, block), lambda i, j, k: (i, j)),
        out_shape=jax.ShapeDtypeStruct((columns, columns), jnp.float32),
        compiler_params=pltpu.CompilerParams(vmem_limit_bytes=VMEM_BYTES),
    )(values, values)


def on_device(panel, response):
    col_rows, epoch_count = panel.shape
    tm_count = lax.axis_size("tm")
    total_len = tm_count * epoch_count
    tables = tuple(jnp.asarray(table) for table in make_tables(total_len))
    gains = gain_tables(response, total_len)
    grouped = panel.reshape(tm_count, col_rows // tm_count, epoch_count // INNER, INNER)
    series = lax.all_to_all(grouped, "tm", split_axis=0, concat_axis=0, tiled=True)
    filtered = filter_columns(series, tables, gains)
    landed = lax.all_to_all(filtered, ("col", "tm"), split_axis=0, concat_axis=1, tiled=True)
    partial_sum = gram(landed, INNER / total_len / total_len)
    summed = lax.psum_scatter(partial_sum, "col", scatter_dimension=0, tiled=True)
    return lax.psum_scatter(summed, "tm", scatter_dimension=1, tiled=True)


def solution(mesh):
    in_specs = (P("col", "tm"), P())
    out_specs = P("col", "tm")
    return jax.shard_map(
        on_device, mesh=mesh, in_specs=in_specs, out_specs=out_specs, check_vma=False
    )
```

```python
import functools
import math

import jax
import jax.numpy as jnp
import numpy as np
from jax import lax
from jax.experimental import pallas as pl
from jax.experimental.pallas import tpu as pltpu
from jax.sharding import PartitionSpec as P

INNER = 256
LANES = 128
VMEM_BYTES = 58 * 1024 * 1024


def split_table(table):
    upper = np.asarray(table, np.float32).astype(jnp.bfloat16)
    lower = (np.asarray(table, np.float64) - upper.astype(np.float64)).astype(jnp.bfloat16)
    return np.stack([upper, lower])


def make_tables(total_len):
    outer = total_len // INNER
    half = outer // 2
    row = np.arange(half)[:, None]
    angle = 2.0 * math.pi * (row * np.arange(outer)[None, :] % outer) / outer
    cosine, sine = np.cos(angle), -np.sin(angle)
    sine[0] = 1.0 - 2.0 * (np.arange(outer) % 2)
    first = split_table(np.concatenate([cosine, sine]))
    lane = np.arange(INNER)
    angle = 2.0 * math.pi * (row * lane[None, :] % total_len) / total_len
    twist = np.stack([np.cos(angle), np.sin(angle)]).astype(np.float32)
    angle = 2.0 * math.pi * (lane[:, None] * lane[None, :] % INNER) / INNER
    cosine, sine = np.cos(angle), np.sin(angle)
    inner = split_table(np.block([[cosine, -sine], [sine, cosine]]))
    back = split_table(np.block([[cosine, sine], [-sine, cosine]]))
    return first, twist, inner, back


def gain_tables(response, total_len):
    outer = total_len // INNER
    half = outer // 2
    mirrored = jnp.concatenate([response[:1], jnp.flip(response[1:])])
    gain = 0.5 * (response + mirrored)
    grid = gain.reshape(INNER, outer).T
    wide = jnp.tile(grid[:half] * (math.sqrt(2.0) / INNER), (1, 2))
    lane = np.arange(INNER)
    blocks = []
    for shift, channel in ((0, 0), (1, half)):
        angle = math.pi * (lane[:, None] * (2 * lane[None, :] + shift) % (2 * INNER)) / INNER
        basis = np.concatenate([np.cos(angle), np.sin(angle)], axis=1).astype(np.float32)
        scaled = basis * jnp.tile(grid[channel] / INNER, 2)[None, :]
        blocks.append(jnp.dot(scaled, basis.T, precision=lax.Precision.HIGHEST))
    zero = jnp.zeros_like(blocks[0])
    edge = jnp.concatenate(
        [jnp.concatenate([blocks[0], zero], axis=1), jnp.concatenate([zero, blocks[1]], axis=1)]
    )
    upper = edge.astype(jnp.bfloat16)
    lower = (edge - upper.astype(jnp.float32)).astype(jnp.bfloat16)
    return wide, jnp.stack([upper, lower])


def product(left, right):
    return jnp.dot(left, right, preferred_element_type=jnp.float32)


def outer_stage(values, first, twist, mixed, index, count):
    half = twist.shape[1]
    sums = product(first[0], values) + product(first[1], values)
    real, imag = sums[:half], sums[half:]
    cosine, sine = twist[0], twist[1]
    turned = (real * cosine + imag * sine, imag * cosine - real * sine)
    for piece in range(2 * INNER // LANES):
        part, lane = divmod(piece * LANES, INNER)
        mixed.at[piece][pl.ds(index, half, stride=count), :] = turned[part][:, lane : lane + LANES]


def mixed_rows(mixed, start, size):
    return jnp.concatenate([mixed[piece, pl.ds(start, size), :] for piece in range(mixed.shape[0])], axis=1)


def inner_stage(values, gain, inner, back):
    rows = values.astype(jnp.bfloat16)
    spectrum = product(rows, inner[0]) + product(rows, inner[1])
    channels = gain.shape[0]
    spectrum = spectrum.reshape(channels, -1, 2 * INNER) * gain[:, None, :]
    spectrum = spectrum.reshape(-1, 2 * INNER)
    upper = spectrum.astype(jnp.bfloat16)
    lower = (spectrum - upper.astype(jnp.float32)).astype(jnp.bfloat16)
    return product(upper, back[0]) + product(lower, back[0]) + product(upper, back[1])


def edge_stage(values, edge):
    rows = values.astype(jnp.bfloat16)
    return product(rows, edge[0]) + product(rows, edge[1])


MESH = pl.DeviceIdType.MESH


def whiten_gram_kernel(
    panel_ref, first_ref, twist_ref, inner_ref, back_ref, gain_ref, edge_ref, out_ref,
    series, mixed, staged, landed, send_in, recv_in, send_out, recv_out, local_sem,
    *, tm_count, col_count, scale,
):
    my_tm, my_col = lax.axis_index("tm"), lax.axis_index("col")
    me = my_col * tm_count + my_tm
    devices = tm_count * col_count
    chunks, _, count, steps, _ = series.shape
    half = twist_ref.shape[1]
    share = half // devices

    barrier = pltpu.get_barrier_semaphore()

    @pl.loop(1, devices)
    def _(offset):
        peer = lax.rem(me + offset, devices)
        there = {"tm": lax.rem(peer, tm_count), "col": peer // tm_count}
        pl.semaphore_signal(barrier, inc=1, device_id=there, device_id_type=MESH)

    pl.semaphore_wait(barrier, devices - 1)

    def copy_in(chunk, target, sender):
        return pltpu.make_async_remote_copy(
            src_ref=panel_ref.at[target, pl.ds(chunk * count, count)],
            dst_ref=series.at[chunk, sender],
            send_sem=send_in.at[chunk, target],
            recv_sem=recv_in.at[chunk, sender],
            device_id={"tm": target, "col": my_col},
            device_id_type=MESH,
        )

    def keep_in(chunk):
        return pltpu.make_async_copy(
            panel_ref.at[my_tm, pl.ds(chunk * count, count)], series.at[chunk, my_tm], local_sem.at[0, chunk]
        )

    def copy_out(chunk, target, sender):
        return pltpu.make_async_remote_copy(
            src_ref=staged.at[chunk, pl.ds(target * share, share)],
            dst_ref=landed.at[:, sender, chunk],
            send_sem=send_out.at[chunk, target],
            recv_sem=recv_out.at[chunk, sender],
            device_id={"tm": lax.rem(target, tm_count), "col": target // tm_count},
            device_id_type=MESH,
        )

    def keep_out(chunk):
        return pltpu.make_async_copy(
            staged.at[chunk, pl.ds(me * share, share)], landed.at[:, me, chunk], local_sem.at[1, chunk]
        )

    def start_in(chunk):
        @pl.loop(1, tm_count)
        def _(offset):
            copy_in(chunk, lax.rem(my_tm + offset, tm_count), my_tm).start()

        keep_in(chunk).start()

    start_in(0)
    channels = max(share, min(half, 32))
    targets = channels // share
    tiles = half // channels

    @pl.loop(0, chunks)
    def _(chunk):
        @pl.loop(1, tm_count)
        def _(offset):
            peer = lax.rem(my_tm + offset, tm_count)
            copy_in(chunk, peer, peer).wait_recv()

        keep_in(chunk).wait()

        @pl.when(chunk + 1 < chunks)
        def _():
            start_in(chunk + 1)

        @pl.loop(0, count)
        def _(index):
            values = series[chunk, :, index].reshape(tm_count * steps, INNER)
            outer_stage(values, first_ref, twist_ref, mixed, index, count)

        @pl.loop(0, tiles)
        def _(turn):
            tile = lax.rem((my_col + 1) * (tiles // col_count) + turn, tiles)
            start = pl.multiple_of(tile * channels, channels)
            rows = mixed_rows(mixed, start * count, channels * count)
            result = inner_stage(rows, gain_ref[pl.ds(start, channels), :], inner_ref, back_ref)
            staged[chunk, pl.ds(start, channels)] = result.reshape(channels, count, 2 * INNER).astype(
                staged.dtype
            )

            @pl.when(tile == 0)
            def _():
                staged[chunk, 0] = edge_stage(mixed_rows(mixed, 0, count), edge_ref).astype(staged.dtype)

            @pl.loop(0, targets)
            def _(place):
                target = tile * targets + lax.rem(place + my_tm, targets)

                @pl.when(target != me)
                def _():
                    copy_out(chunk, target, me).start()

                @pl.when(target == me)
                def _():
                    keep_out(chunk).start()

    @pl.loop(0, chunks)
    def _(chunk):
        @pl.loop(1, devices)
        def _(offset):
            peer = lax.rem(me + offset, devices)
            copy_out(chunk, peer, peer).wait_recv()

        keep_out(chunk).wait()

    width = out_ref.shape[2]
    col_rows = tm_count * chunks * count
    parts = col_rows // width

    @pl.loop(0, col_count * col_count)
    def _(block):
        i, j = block // col_count, lax.rem(block, col_count)
        total = jnp.zeros((col_rows, col_rows), jnp.float32)
        for channel in range(share):
            left = landed[channel, pl.ds(i * tm_count, tm_count)].reshape(col_rows, 2 * INNER)
            right = landed[channel, pl.ds(j * tm_count, tm_count)].reshape(col_rows, 2 * INNER)
            total = total + lax.dot_general(
                left, right, (((1,), (1,)), ((), ())), preferred_element_type=jnp.float32
            )
        total = total * scale
        for part in range(parts):
            out_ref[j * parts + part, pl.ds(pl.multiple_of(i * col_rows, col_rows), col_rows), :] = total[
                :, part * width : (part + 1) * width
            ]

    @pl.loop(0, chunks)
    def _(chunk):
        @pl.loop(1, tm_count)
        def _(offset):
            copy_in(chunk, lax.rem(my_tm + offset, tm_count), my_tm).wait_send()

        @pl.loop(1, devices)
        def _(offset):
            copy_out(chunk, lax.rem(me + offset, devices), me).wait_send()


def whiten_gram(grouped, tables, gains, col_count, scale):
    first, twist, inner, back = tables
    gain, edge = gains
    tm_count, per_device, steps, _ = grouped.shape
    half = twist.shape[1]
    count = math.gcd(per_device, 16)
    chunks = per_device // count
    devices = tm_count * col_count
    columns = devices * per_device
    vmem = pl.BlockSpec(memory_space=pltpu.VMEM)
    return pl.pallas_call(
        functools.partial(whiten_gram_kernel, tm_count=tm_count, col_count=col_count, scale=scale),
        in_specs=[pl.BlockSpec(memory_space=pl.ANY)] + [vmem] * 6,
        out_specs=vmem,
        out_shape=jax.ShapeDtypeStruct((tm_count, columns, columns // tm_count), jnp.float32),
        scratch_shapes=[
            pltpu.VMEM((chunks, tm_count, count, steps, INNER), jnp.bfloat16),
            pltpu.VMEM((2 * INNER // LANES, half * count, LANES), jnp.float32),
            pltpu.VMEM((chunks, half, count, 2 * INNER), jnp.bfloat16),
            pltpu.VMEM((half // devices, devices, chunks, count, 2 * INNER), jnp.bfloat16),
            pltpu.SemaphoreType.DMA((chunks, tm_count)),
            pltpu.SemaphoreType.DMA((chunks, tm_count)),
            pltpu.SemaphoreType.DMA((chunks, devices)),
            pltpu.SemaphoreType.DMA((chunks, devices)),
            pltpu.SemaphoreType.DMA((2, chunks)),
        ],
        compiler_params=pltpu.CompilerParams(
            collective_id=0, has_side_effects=True, vmem_limit_bytes=VMEM_BYTES
        ),
    )(grouped, first, twist, inner, back, gain, edge)


def on_device(panel, response):
    col_rows, epoch_count = panel.shape
    tm_count = lax.axis_size("tm")
    total_len = tm_count * epoch_count
    tables = tuple(jnp.asarray(table) for table in make_tables(total_len))
    gains = gain_tables(response, total_len)
    grouped = panel.reshape(tm_count, col_rows // tm_count, epoch_count // INNER, INNER)
    col_count = lax.axis_size("col")
    partial_sum = whiten_gram(grouped, tables, gains, col_count, INNER / total_len / total_len)
    across = lax.all_to_all(partial_sum, "tm", split_axis=0, concat_axis=0, tiled=True)
    summed = jnp.sum(across, axis=0).reshape(col_count, col_rows, -1)
    return jnp.sum(lax.all_to_all(summed, "col", split_axis=0, concat_axis=0, tiled=True), axis=0)


def solution(mesh):
    in_specs = (P("col", "tm"), P())
    out_specs = P("col", "tm")
    return jax.shard_map(
        on_device, mesh=mesh, in_specs=in_specs, out_specs=out_specs, check_vma=False
    )
```

```python
import functools
import math

import jax
import jax.numpy as jnp
import numpy as np
from jax import lax
from jax.experimental import pallas as pl
from jax.experimental.pallas import tpu as pltpu
from jax.sharding import PartitionSpec as P

INNER = 256
LANES = 128
PAIR = 2
VMEM_BYTES = 58 * 1024 * 1024


def split_table(table):
    upper = np.asarray(table, np.float32).astype(jnp.bfloat16)
    lower = (np.asarray(table, np.float64) - upper.astype(np.float64)).astype(jnp.bfloat16)
    return np.stack([upper, lower])


def make_tables(total_len):
    outer = total_len // INNER
    half = outer // 2
    row = np.arange(half)[:, None]
    angle = 2.0 * math.pi * (row * np.arange(outer)[None, :] % outer) / outer
    cosine, sine = np.cos(angle), -np.sin(angle)
    sine[0] = 1.0 - 2.0 * (np.arange(outer) % 2)
    first = split_table(np.concatenate([cosine, sine]))
    lane = np.arange(INNER)
    angle = 2.0 * math.pi * (row * lane[None, :] % total_len) / total_len
    twist = np.stack([np.cos(angle), np.sin(angle)]).astype(np.float32)
    angle = 2.0 * math.pi * (lane[:, None] * lane[None, :] % INNER) / INNER
    cosine, sine = np.cos(angle), np.sin(angle)
    inner = split_table(np.block([[cosine, -sine], [sine, cosine]]))
    back = split_table(np.block([[cosine, sine], [-sine, cosine]]))
    return first, twist, inner, back


def gain_tables(response, total_len):
    outer = total_len // INNER
    half = outer // 2
    mirrored = jnp.concatenate([response[:1], jnp.flip(response[1:])])
    gain = 0.5 * (response + mirrored)
    grid = gain.reshape(INNER, outer).T
    wide = jnp.tile(grid[:half] * (math.sqrt(2.0) / INNER), (1, 2))
    lane = np.arange(INNER)
    blocks = []
    for shift, channel in ((0, 0), (1, half)):
        angle = math.pi * (lane[:, None] * (2 * lane[None, :] + shift) % (2 * INNER)) / INNER
        basis = np.concatenate([np.cos(angle), np.sin(angle)], axis=1).astype(np.float32)
        scaled = basis * jnp.tile(grid[channel] / INNER, 2)[None, :]
        blocks.append(jnp.dot(scaled, basis.T, precision=lax.Precision.HIGHEST))
    zero = jnp.zeros_like(blocks[0])
    edge = jnp.concatenate(
        [jnp.concatenate([blocks[0], zero], axis=1), jnp.concatenate([zero, blocks[1]], axis=1)]
    )
    upper = edge.astype(jnp.bfloat16)
    lower = (edge - upper.astype(jnp.float32)).astype(jnp.bfloat16)
    return wide, jnp.stack([upper, lower])


def product(left, right):
    return jnp.dot(left, right, preferred_element_type=jnp.float32)


def outer_stage(values, first, twist, mixed, index, count):
    half = twist.shape[1]
    sums = product(first[0], values) + product(first[1], values)
    real, imag = sums[:half], sums[half:]
    cosine, sine = twist[0], twist[1]
    turned = (real * cosine + imag * sine, imag * cosine - real * sine)
    for piece in range(2 * INNER // LANES):
        part, lane = divmod(piece * LANES, INNER)
        mixed.at[piece][pl.ds(index, half, stride=count), :] = turned[part][:, lane : lane + LANES]


def mixed_rows(mixed, start, size):
    return jnp.concatenate([mixed[piece, pl.ds(start, size), :] for piece in range(mixed.shape[0])], axis=1)


def inner_stage(values, gain, inner, back):
    rows = values.astype(jnp.bfloat16)
    spectrum = product(rows, inner[0]) + product(rows, inner[1])
    channels = gain.shape[0]
    spectrum = spectrum.reshape(channels, -1, 2 * INNER) * gain[:, None, :]
    spectrum = spectrum.reshape(-1, 2 * INNER)
    upper = spectrum.astype(jnp.bfloat16)
    lower = (spectrum - upper.astype(jnp.float32)).astype(jnp.bfloat16)
    return product(upper, back[0]) + product(lower, back[0]) + product(upper, back[1])


def edge_stage(values, edge):
    rows = values.astype(jnp.bfloat16)
    return product(rows, edge[0]) + product(rows, edge[1])


MESH = pl.DeviceIdType.MESH


def whiten_gram_kernel(
    panel_ref, first_ref, twist_ref, inner_ref, back_ref, gain_ref, edge_ref, out_ref,
    series, mixed, staged, landed, partial, pair_land, plane_land, summed, line_land,
    send_in, recv_in, send_out, recv_out, local_sem,
    send_pair, recv_pair, send_plane, recv_plane, send_line, recv_line,
    *, tm_count, col_count, scale,
):
    my_tm, my_col = lax.axis_index("tm"), lax.axis_index("col")
    me = my_col * tm_count + my_tm
    devices = tm_count * col_count
    chunks, _, count, steps, _ = series.shape
    half = twist_ref.shape[1]
    share = half // devices

    barrier = pltpu.get_barrier_semaphore()

    @pl.loop(1, devices)
    def _(offset):
        peer = lax.rem(me + offset, devices)
        there = {"tm": lax.rem(peer, tm_count), "col": peer // tm_count}
        pl.semaphore_signal(barrier, inc=1, device_id=there, device_id_type=MESH)

    pl.semaphore_wait(barrier, devices - 1)

    def copy_in(chunk, target, sender):
        return pltpu.make_async_remote_copy(
            src_ref=panel_ref.at[target, pl.ds(chunk * count, count)],
            dst_ref=series.at[chunk, sender],
            send_sem=send_in.at[chunk, target],
            recv_sem=recv_in.at[chunk, sender],
            device_id={"tm": target, "col": my_col},
            device_id_type=MESH,
        )

    def keep_in(chunk):
        return pltpu.make_async_copy(
            panel_ref.at[my_tm, pl.ds(chunk * count, count)], series.at[chunk, my_tm], local_sem.at[0, chunk]
        )

    def copy_out(chunk, target, sender):
        return pltpu.make_async_remote_copy(
            src_ref=staged.at[chunk, pl.ds(target * share, share)],
            dst_ref=landed.at[:, sender, chunk],
            send_sem=send_out.at[chunk, target],
            recv_sem=recv_out.at[chunk, sender],
            device_id={"tm": lax.rem(target, tm_count), "col": target // tm_count},
            device_id_type=MESH,
        )

    def keep_out(chunk):
        return pltpu.make_async_copy(
            staged.at[chunk, pl.ds(me * share, share)], landed.at[:, me, chunk], local_sem.at[1, chunk]
        )

    def start_in(chunk):
        @pl.loop(1, tm_count)
        def _(offset):
            copy_in(chunk, lax.rem(my_tm + offset, tm_count), my_tm).start()

        keep_in(chunk).start()

    start_in(0)
    channels = max(share, min(half, 32))
    targets = channels // share
    tiles = half // channels

    @pl.loop(0, chunks)
    def _(chunk):
        @pl.loop(1, tm_count)
        def _(offset):
            peer = lax.rem(my_tm + offset, tm_count)
            copy_in(chunk, peer, peer).wait_recv()

        keep_in(chunk).wait()

        @pl.when(chunk + 1 < chunks)
        def _():
            start_in(chunk + 1)

        @pl.loop(0, count)
        def _(index):
            values = series[chunk, :, index].reshape(tm_count * steps, INNER)
            outer_stage(values, first_ref, twist_ref, mixed, index, count)

        @pl.loop(0, tiles)
        def _(turn):
            tile = lax.rem((my_col + 1) * (tiles // col_count) + turn, tiles)
            start = pl.multiple_of(tile * channels, channels)
            rows = mixed_rows(mixed, start * count, channels * count)
            result = inner_stage(rows, gain_ref[pl.ds(start, channels), :], inner_ref, back_ref)
            staged[chunk, pl.ds(start, channels)] = result.reshape(channels, count, 2 * INNER).astype(
                staged.dtype
            )

            @pl.when(tile == 0)
            def _():
                staged[chunk, 0] = edge_stage(mixed_rows(mixed, 0, count), edge_ref).astype(staged.dtype)

            @pl.loop(0, targets)
            def _(place):
                target = tile * targets + lax.rem(place + my_tm, targets)

                @pl.when(target != me)
                def _():
                    copy_out(chunk, target, me).start()

                @pl.when(target == me)
                def _():
                    keep_out(chunk).start()

    @pl.loop(0, chunks)
    def _(chunk):
        @pl.loop(1, devices)
        def _(offset):
            peer = lax.rem(me + offset, devices)
            copy_out(chunk, peer, peer).wait_recv()

        keep_out(chunk).wait()

    col_rows, width = out_ref.shape
    parts = col_rows // width
    chips = tm_count // PAIR
    my_chip, my_core = my_tm // PAIR, lax.rem(my_tm, PAIR)
    other_core = PAIR - 1 - my_core

    def pair_copy(row):
        return pltpu.make_async_remote_copy(
            src_ref=partial.at[row, other_core],
            dst_ref=pair_land.at[row],
            send_sem=send_pair.at[row],
            recv_sem=recv_pair.at[row],
            device_id={"tm": my_chip * PAIR + other_core, "col": my_col},
            device_id_type=MESH,
        )

    def plane_copy(row, target, sender):
        return pltpu.make_async_remote_copy(
            src_ref=partial.at[row, my_core, target],
            dst_ref=plane_land.at[row, sender],
            send_sem=send_plane.at[row, target],
            recv_sem=recv_plane.at[row, sender],
            device_id={"tm": target * PAIR + my_core, "col": my_col},
            device_id_type=MESH,
        )

    def line_copy(target, sender):
        return pltpu.make_async_remote_copy(
            src_ref=summed.at[target],
            dst_ref=line_land.at[sender],
            send_sem=send_line.at[target],
            recv_sem=recv_line.at[sender],
            device_id={"tm": my_tm, "col": target},
            device_id_type=MESH,
        )

    @pl.loop(0, col_count + 2)
    def _(step):
        @pl.when(step < col_count)
        def _():
            row = lax.rem(my_col + 1 + step, col_count)

            @pl.loop(0, col_count)
            def _(j):
                total = jnp.zeros((col_rows, col_rows), jnp.float32)
                for channel in range(share):
                    left = landed[channel, pl.ds(row * tm_count, tm_count)].reshape(col_rows, 2 * INNER)
                    right = landed[channel, pl.ds(j * tm_count, tm_count)].reshape(col_rows, 2 * INNER)
                    total = total + lax.dot_general(
                        left, right, (((1,), (1,)), ((), ())), preferred_element_type=jnp.float32
                    )
                total = total * scale
                for part in range(parts):
                    owner = j * parts + part
                    partial[row, lax.rem(owner, PAIR), owner // PAIR] = total[:, part * width : (part + 1) * width]

            pair_copy(row).start()

        @pl.when((step >= 1) & (step < col_count + 1))
        def _():
            row = lax.rem(my_col + step, col_count)
            pair_copy(row).wait_recv()
            partial[row, my_core] = partial[row, my_core] + pair_land[row]

            @pl.loop(1, chips)
            def _(offset):
                plane_copy(row, lax.rem(my_chip + offset, chips), my_chip).start()

        @pl.when(step >= 2)
        def _():
            row = lax.rem(my_col + step - 1, col_count)
            summed[row] = partial[row, my_core, my_chip]

            @pl.loop(1, chips)
            def _(offset):
                peer = lax.rem(my_chip + offset, chips)
                plane_copy(row, peer, peer).wait_recv()
                summed[row] = summed[row] + plane_land[row, peer]

            @pl.when(row != my_col)
            def _():
                line_copy(row, my_col).start()

    out_ref[...] = summed[my_col]

    @pl.loop(1, col_count)
    def _(offset):
        peer = lax.rem(my_col + offset, col_count)
        line_copy(peer, peer).wait_recv()
        out_ref[...] = out_ref[...] + line_land[peer]

    @pl.loop(0, col_count)
    def _(row):
        pair_copy(row).wait_send()

        @pl.loop(1, chips)
        def _(offset):
            plane_copy(row, lax.rem(my_chip + offset, chips), my_chip).wait_send()

        @pl.when(row != my_col)
        def _():
            line_copy(row, my_col).wait_send()

    @pl.loop(0, chunks)
    def _(chunk):
        @pl.loop(1, tm_count)
        def _(offset):
            copy_in(chunk, lax.rem(my_tm + offset, tm_count), my_tm).wait_send()

        @pl.loop(1, devices)
        def _(offset):
            copy_out(chunk, lax.rem(me + offset, devices), me).wait_send()


def whiten_gram(grouped, tables, gains, col_count, scale):
    first, twist, inner, back = tables
    gain, edge = gains
    tm_count, per_device, steps, _ = grouped.shape
    half = twist.shape[1]
    count = math.gcd(per_device, 16)
    chunks = per_device // count
    devices = tm_count * col_count
    columns = devices * per_device
    chips = tm_count // PAIR
    block = (columns // col_count, columns // tm_count)
    vmem = pl.BlockSpec(memory_space=pltpu.VMEM)
    return pl.pallas_call(
        functools.partial(whiten_gram_kernel, tm_count=tm_count, col_count=col_count, scale=scale),
        in_specs=[pl.BlockSpec(memory_space=pl.ANY)] + [vmem] * 6,
        out_specs=vmem,
        out_shape=jax.ShapeDtypeStruct(block, jnp.float32),
        scratch_shapes=[
            pltpu.VMEM((chunks, tm_count, count, steps, INNER), jnp.bfloat16),
            pltpu.VMEM((2 * INNER // LANES, half * count, LANES), jnp.float32),
            pltpu.VMEM((chunks, half, count, 2 * INNER), jnp.bfloat16),
            pltpu.VMEM((half // devices, devices, chunks, count, 2 * INNER), jnp.bfloat16),
            pltpu.VMEM((col_count, PAIR, chips, *block), jnp.float32),
            pltpu.VMEM((col_count, chips, *block), jnp.float32),
            pltpu.VMEM((col_count, chips, *block), jnp.float32),
            pltpu.VMEM((col_count, *block), jnp.float32),
            pltpu.VMEM((col_count, *block), jnp.float32),
            pltpu.SemaphoreType.DMA((chunks, tm_count)),
            pltpu.SemaphoreType.DMA((chunks, tm_count)),
            pltpu.SemaphoreType.DMA((chunks, devices)),
            pltpu.SemaphoreType.DMA((chunks, devices)),
            pltpu.SemaphoreType.DMA((2, chunks)),
            pltpu.SemaphoreType.DMA((col_count,)),
            pltpu.SemaphoreType.DMA((col_count,)),
            pltpu.SemaphoreType.DMA((col_count, chips)),
            pltpu.SemaphoreType.DMA((col_count, chips)),
            pltpu.SemaphoreType.DMA((col_count,)),
            pltpu.SemaphoreType.DMA((col_count,)),
        ],
        compiler_params=pltpu.CompilerParams(
            collective_id=0, has_side_effects=True, vmem_limit_bytes=VMEM_BYTES
        ),
    )(grouped, first, twist, inner, back, gain, edge)


def on_device(panel, response):
    col_rows, epoch_count = panel.shape
    tm_count = lax.axis_size("tm")
    total_len = tm_count * epoch_count
    tables = tuple(jnp.asarray(table) for table in make_tables(total_len))
    gains = gain_tables(response, total_len)
    grouped = panel.reshape(tm_count, col_rows // tm_count, epoch_count // INNER, INNER)
    col_count = lax.axis_size("col")
    return whiten_gram(grouped, tables, gains, col_count, INNER / total_len / total_len)


def solution(mesh):
    in_specs = (P("col", "tm"), P())
    out_specs = P("col", "tm")
    return jax.shard_map(
        on_device, mesh=mesh, in_specs=in_specs, out_specs=out_specs, check_vma=False
    )
```

```python
import functools
import math

import jax
import jax.numpy as jnp
import numpy as np
from jax import lax
from jax.experimental import pallas as pl
from jax.experimental.pallas import tpu as pltpu
from jax.sharding import PartitionSpec as P

INNER = 256
LANES = 128
PAIR = 2
VMEM_BYTES = 58 * 1024 * 1024


def split_table(table):
    upper = np.asarray(table, np.float32).astype(jnp.bfloat16)
    lower = (np.asarray(table, np.float64) - upper.astype(np.float64)).astype(jnp.bfloat16)
    return np.stack([upper, lower])


def make_tables(total_len):
    outer = total_len // INNER
    half = outer // 2
    row = np.arange(half)[:, None]
    angle = 2.0 * math.pi * (row * np.arange(outer)[None, :] % outer) / outer
    cosine, sine = np.cos(angle), -np.sin(angle)
    sine[0] = 1.0 - 2.0 * (np.arange(outer) % 2)
    first = split_table(np.concatenate([cosine, sine]))
    lane = np.arange(INNER)
    angle = 2.0 * math.pi * (row * lane[None, :] % total_len) / total_len
    twist = np.stack([np.cos(angle), np.sin(angle)]).astype(np.float32)
    angle = 2.0 * math.pi * (lane[:, None] * lane[None, :] % INNER) / INNER
    cosine, sine = np.cos(angle), np.sin(angle)
    inner = split_table(np.block([[cosine, -sine], [sine, cosine]]))
    back = split_table(np.block([[cosine, sine], [-sine, cosine]]))
    angle = math.pi * lane / INNER
    turn = np.stack([np.cos(angle), np.sin(angle)]).astype(np.float32)
    return first, twist, inner, back, turn


def gain_tables(response, total_len):
    outer = total_len // INNER
    half = outer // 2
    mirrored = jnp.concatenate([response[:1], jnp.flip(response[1:])])
    gain = 0.5 * (response + mirrored)
    grid = gain.reshape(INNER, outer).T
    wide = jnp.tile(grid[:half] * (math.sqrt(2.0) / INNER), (1, 2))
    edge = jnp.tile(jnp.stack([grid[0], grid[half]]) * (1.0 / INNER), (1, 2))
    return wide, edge


def product(left, right):
    return jnp.dot(left, right, preferred_element_type=jnp.float32)


def outer_stage(values, first, twist, mixed, index, count):
    half = twist.shape[1]
    sums = product(first[0], values) + product(first[1], values)
    real, imag = sums[:half], sums[half:]
    cosine, sine = twist[0], twist[1]
    turned = (real * cosine + imag * sine, imag * cosine - real * sine)
    for piece in range(2 * INNER // LANES):
        part, lane = divmod(piece * LANES, INNER)
        mixed.at[piece][pl.ds(index, half, stride=count), :] = turned[part][:, lane : lane + LANES]


def mixed_rows(mixed, start, size):
    return jnp.concatenate([mixed[piece, pl.ds(start, size), :] for piece in range(mixed.shape[0])], axis=1)


def inner_stage(values, gain, inner, back):
    rows = values.astype(jnp.bfloat16)
    spectrum = product(rows, inner[0]) + product(rows, inner[1])
    channels = gain.shape[0]
    spectrum = spectrum.reshape(channels, -1, 2 * INNER) * gain[:, None, :]
    spectrum = spectrum.reshape(-1, 2 * INNER)
    upper = spectrum.astype(jnp.bfloat16)
    lower = (spectrum - upper.astype(jnp.float32)).astype(jnp.bfloat16)
    return product(upper, back[0]) + product(lower, back[0]) + product(upper, back[1])


def edge_stage(values, gain, inner, back, turn):
    low, high = values[:, :INNER], values[:, INNER:]
    cosine, sine = turn[0:1], turn[1:2]
    rows = jnp.concatenate(
        [
            jnp.concatenate([low, jnp.zeros_like(low)], axis=1),
            jnp.concatenate([high * cosine, -high * sine], axis=1),
        ]
    )
    result = inner_stage(rows, gain, inner, back)
    size = values.shape[0]
    low = result[:size, :INNER]
    high = result[size:, :INNER] * cosine - result[size:, INNER:] * sine
    return jnp.concatenate([low, high], axis=1)


MESH = pl.DeviceIdType.MESH


def whiten_gram_kernel(
    panel_ref, first_ref, twist_ref, inner_ref, back_ref, gain_ref, edge_ref, turn_ref, out_ref,
    series, mixed, staged, landed, partial, pair_land, plane_land, summed, line_land,
    send_in, recv_in, send_out, recv_out, local_sem,
    send_pair, recv_pair, send_plane, recv_plane, send_line, recv_line,
    *, tm_count, col_count, scale,
):
    my_tm, my_col = lax.axis_index("tm"), lax.axis_index("col")
    me = my_col * tm_count + my_tm
    devices = tm_count * col_count
    chunks, _, count, steps, _ = series.shape
    half = twist_ref.shape[1]
    share = half // devices

    barrier = pltpu.get_barrier_semaphore()

    @pl.loop(1, devices)
    def _(offset):
        peer = lax.rem(me + offset, devices)
        there = {"tm": lax.rem(peer, tm_count), "col": peer // tm_count}
        pl.semaphore_signal(barrier, inc=1, device_id=there, device_id_type=MESH)

    pl.semaphore_wait(barrier, devices - 1)

    def copy_in(chunk, target, sender):
        return pltpu.make_async_remote_copy(
            src_ref=panel_ref.at[target, pl.ds(chunk * count, count)],
            dst_ref=series.at[chunk, sender],
            send_sem=send_in.at[chunk, target],
            recv_sem=recv_in.at[chunk, sender],
            device_id={"tm": target, "col": my_col},
            device_id_type=MESH,
        )

    def keep_in(chunk):
        return pltpu.make_async_copy(
            panel_ref.at[my_tm, pl.ds(chunk * count, count)], series.at[chunk, my_tm], local_sem.at[0, chunk]
        )

    def copy_out(chunk, target, sender):
        return pltpu.make_async_remote_copy(
            src_ref=staged.at[chunk, pl.ds(target * share, share)],
            dst_ref=landed.at[:, sender, chunk],
            send_sem=send_out.at[chunk, target],
            recv_sem=recv_out.at[chunk, sender],
            device_id={"tm": lax.rem(target, tm_count), "col": target // tm_count},
            device_id_type=MESH,
        )

    def keep_out(chunk):
        return pltpu.make_async_copy(
            staged.at[chunk, pl.ds(me * share, share)], landed.at[:, me, chunk], local_sem.at[1, chunk]
        )

    def start_in(chunk):
        @pl.loop(1, tm_count)
        def _(offset):
            copy_in(chunk, lax.rem(my_tm + offset, tm_count), my_tm).start()

        keep_in(chunk).start()

    start_in(0)
    channels = max(share, min(half, 32))
    targets = channels // share
    tiles = half // channels

    @pl.loop(0, chunks)
    def _(chunk):
        @pl.loop(1, tm_count)
        def _(offset):
            peer = lax.rem(my_tm + offset, tm_count)
            copy_in(chunk, peer, peer).wait_recv()

        keep_in(chunk).wait()

        @pl.when(chunk + 1 < chunks)
        def _():
            start_in(chunk + 1)

        @pl.loop(0, count)
        def _(index):
            values = series[chunk, :, index].reshape(tm_count * steps, INNER)
            outer_stage(values, first_ref, twist_ref, mixed, index, count)

        @pl.loop(0, tiles)
        def _(turn):
            per_side = tiles // 2
            side = lax.rem(my_col // (col_count // 2) + 1 + turn // per_side, 2)
            shift = lax.rem(my_col, col_count // 2) * (tiles // col_count)
            tile = side * per_side + lax.rem(turn + shift, per_side)
            start = pl.multiple_of(tile * channels, channels)
            rows = mixed_rows(mixed, start * count, channels * count)
            result = inner_stage(rows, gain_ref[pl.ds(start, channels), :], inner_ref, back_ref)
            staged[chunk, pl.ds(start, channels)] = result.reshape(channels, count, 2 * INNER).astype(
                staged.dtype
            )

            @pl.when(tile == 0)
            def _():
                staged[chunk, 0] = edge_stage(
                    mixed_rows(mixed, 0, count), edge_ref[...], inner_ref, back_ref, turn_ref
                ).astype(staged.dtype)

            @pl.loop(0, targets)
            def _(place):
                target = tile * targets + lax.rem(place + my_tm, targets)

                @pl.when(target != me)
                def _():
                    copy_out(chunk, target, me).start()

                @pl.when(target == me)
                def _():
                    keep_out(chunk).start()

    @pl.loop(0, chunks)
    def _(chunk):
        @pl.loop(1, devices)
        def _(offset):
            peer = lax.rem(me + offset, devices)
            copy_out(chunk, peer, peer).wait_recv()

        keep_out(chunk).wait()

    col_rows, width = out_ref.shape
    parts = col_rows // width
    chips = tm_count // PAIR
    my_chip, my_core = my_tm // PAIR, lax.rem(my_tm, PAIR)
    other_core = PAIR - 1 - my_core

    def pair_copy(row):
        return pltpu.make_async_remote_copy(
            src_ref=partial.at[row, other_core],
            dst_ref=pair_land.at[row],
            send_sem=send_pair.at[row],
            recv_sem=recv_pair.at[row],
            device_id={"tm": my_chip * PAIR + other_core, "col": my_col},
            device_id_type=MESH,
        )

    def plane_copy(row, target, sender):
        return pltpu.make_async_remote_copy(
            src_ref=partial.at[row, my_core, target],
            dst_ref=plane_land.at[row, sender],
            send_sem=send_plane.at[row, target],
            recv_sem=recv_plane.at[row, sender],
            device_id={"tm": target * PAIR + my_core, "col": my_col},
            device_id_type=MESH,
        )

    def line_copy(target, sender):
        return pltpu.make_async_remote_copy(
            src_ref=summed.at[target],
            dst_ref=line_land.at[sender],
            send_sem=send_line.at[target],
            recv_sem=recv_line.at[sender],
            device_id={"tm": my_tm, "col": target},
            device_id_type=MESH,
        )

    @pl.loop(0, col_count + 2)
    def _(step):
        @pl.when(step < col_count)
        def _():
            row = lax.rem(my_col + 1 + step, col_count)

            @pl.loop(0, col_count)
            def _(j):
                total = jnp.zeros((col_rows, col_rows), jnp.float32)
                for channel in range(share):
                    left = landed[channel, pl.ds(row * tm_count, tm_count)].reshape(col_rows, 2 * INNER)
                    right = landed[channel, pl.ds(j * tm_count, tm_count)].reshape(col_rows, 2 * INNER)
                    total = total + lax.dot_general(
                        left, right, (((1,), (1,)), ((), ())), preferred_element_type=jnp.float32
                    )
                total = total * scale
                for part in range(parts):
                    owner = j * parts + part
                    partial[row, lax.rem(owner, PAIR), owner // PAIR] = total[:, part * width : (part + 1) * width]

            pair_copy(row).start()

        @pl.when((step >= 1) & (step < col_count + 1))
        def _():
            row = lax.rem(my_col + step, col_count)
            pair_copy(row).wait_recv()
            partial[row, my_core] = partial[row, my_core] + pair_land[row]

            @pl.loop(1, chips)
            def _(offset):
                plane_copy(row, lax.rem(my_chip + offset, chips), my_chip).start()

        @pl.when(step >= 2)
        def _():
            row = lax.rem(my_col + step - 1, col_count)
            summed[row] = partial[row, my_core, my_chip]

            @pl.loop(1, chips)
            def _(offset):
                peer = lax.rem(my_chip + offset, chips)
                plane_copy(row, peer, peer).wait_recv()
                summed[row] = summed[row] + plane_land[row, peer]

            @pl.when(row != my_col)
            def _():
                line_copy(row, my_col).start()

    out_ref[...] = summed[my_col]

    @pl.loop(1, col_count)
    def _(offset):
        peer = lax.rem(my_col + offset, col_count)
        line_copy(peer, peer).wait_recv()
        out_ref[...] = out_ref[...] + line_land[peer]

    @pl.loop(0, col_count)
    def _(row):
        pair_copy(row).wait_send()

        @pl.loop(1, chips)
        def _(offset):
            plane_copy(row, lax.rem(my_chip + offset, chips), my_chip).wait_send()

        @pl.when(row != my_col)
        def _():
            line_copy(row, my_col).wait_send()

    @pl.loop(0, chunks)
    def _(chunk):
        @pl.loop(1, tm_count)
        def _(offset):
            copy_in(chunk, lax.rem(my_tm + offset, tm_count), my_tm).wait_send()

        @pl.loop(1, devices)
        def _(offset):
            copy_out(chunk, lax.rem(me + offset, devices), me).wait_send()


def whiten_gram(grouped, tables, gains, col_count, scale):
    first, twist, inner, back, turn = tables
    gain, edge = gains
    tm_count, per_device, steps, _ = grouped.shape
    half = twist.shape[1]
    count = math.gcd(per_device, 8)
    chunks = per_device // count
    devices = tm_count * col_count
    columns = devices * per_device
    chips = tm_count // PAIR
    block = (columns // col_count, columns // tm_count)
    vmem = pl.BlockSpec(memory_space=pltpu.VMEM)
    return pl.pallas_call(
        functools.partial(whiten_gram_kernel, tm_count=tm_count, col_count=col_count, scale=scale),
        in_specs=[pl.BlockSpec(memory_space=pl.ANY)] + [vmem] * 7,
        out_specs=vmem,
        out_shape=jax.ShapeDtypeStruct(block, jnp.float32),
        scratch_shapes=[
            pltpu.VMEM((chunks, tm_count, count, steps, INNER), jnp.bfloat16),
            pltpu.VMEM((2 * INNER // LANES, half * count, LANES), jnp.float32),
            pltpu.VMEM((chunks, half, count, 2 * INNER), jnp.bfloat16),
            pltpu.VMEM((half // devices, devices, chunks, count, 2 * INNER), jnp.bfloat16),
            pltpu.VMEM((col_count, PAIR, chips, *block), jnp.float32),
            pltpu.VMEM((col_count, chips, *block), jnp.float32),
            pltpu.VMEM((col_count, chips, *block), jnp.float32),
            pltpu.VMEM((col_count, *block), jnp.float32),
            pltpu.VMEM((col_count, *block), jnp.float32),
            pltpu.SemaphoreType.DMA((chunks, tm_count)),
            pltpu.SemaphoreType.DMA((chunks, tm_count)),
            pltpu.SemaphoreType.DMA((chunks, devices)),
            pltpu.SemaphoreType.DMA((chunks, devices)),
            pltpu.SemaphoreType.DMA((2, chunks)),
            pltpu.SemaphoreType.DMA((col_count,)),
            pltpu.SemaphoreType.DMA((col_count,)),
            pltpu.SemaphoreType.DMA((col_count, chips)),
            pltpu.SemaphoreType.DMA((col_count, chips)),
            pltpu.SemaphoreType.DMA((col_count,)),
            pltpu.SemaphoreType.DMA((col_count,)),
        ],
        compiler_params=pltpu.CompilerParams(
            collective_id=0, has_side_effects=True, vmem_limit_bytes=VMEM_BYTES
        ),
    )(grouped, first, twist, inner, back, gain, edge, turn)


def on_device(panel, response):
    col_rows, epoch_count = panel.shape
    tm_count = lax.axis_size("tm")
    total_len = tm_count * epoch_count
    tables = tuple(jnp.asarray(table) for table in make_tables(total_len))
    gains = gain_tables(response, total_len)
    grouped = panel.reshape(tm_count, col_rows // tm_count, epoch_count // INNER, INNER)
    col_count = lax.axis_size("col")
    return whiten_gram(grouped, tables, gains, col_count, INNER / total_len / total_len)


def solution(mesh):
    in_specs = (P("col", "tm"), P())
    out_specs = P("col", "tm")
    return jax.shard_map(
        on_device, mesh=mesh, in_specs=in_specs, out_specs=out_specs, check_vma=False
    )
```

```python
import functools
import math

import jax
import jax.numpy as jnp
import numpy as np
from jax import lax
from jax.experimental import pallas as pl
from jax.experimental.pallas import tpu as pltpu
from jax.sharding import PartitionSpec as P

INNER = 256
LANES = 128
PAIR = 2
VMEM_BYTES = 58 * 1024 * 1024


def split_table(table):
    upper = np.asarray(table, np.float32).astype(jnp.bfloat16)
    lower = (np.asarray(table, np.float64) - upper.astype(np.float64)).astype(jnp.bfloat16)
    return np.stack([upper, lower])


def make_tables(total_len):
    outer = total_len // INNER
    half = outer // 2
    row = np.arange(half)[:, None]
    angle = 2.0 * math.pi * (row * np.arange(outer)[None, :] % outer) / outer
    cosine, sine = np.cos(angle), -np.sin(angle)
    sine[0] = 1.0 - 2.0 * (np.arange(outer) % 2)
    first = split_table(np.concatenate([cosine, sine]))
    lane = np.arange(INNER)
    angle = 2.0 * math.pi * (row * lane[None, :] % total_len) / total_len
    twist = np.stack([np.cos(angle), np.sin(angle)]).astype(np.float32)
    angle = 2.0 * math.pi * (lane[:, None] * lane[None, :] % INNER) / INNER
    cosine, sine = np.cos(angle), np.sin(angle)
    inner = split_table(np.block([[cosine, -sine], [sine, cosine]]))
    back = split_table(np.block([[cosine, sine], [-sine, cosine]]))
    angle = math.pi * lane / INNER
    turn = np.stack([np.cos(angle), np.sin(angle)]).astype(np.float32)
    return first, twist, inner, back, turn


def gain_tables(response, total_len):
    outer = total_len // INNER
    half = outer // 2
    mirrored = jnp.concatenate([response[:1], jnp.flip(response[1:])])
    gain = 0.5 * (response + mirrored)
    grid = gain.reshape(INNER, outer).T
    wide = jnp.tile(grid[:half] * (math.sqrt(2.0) / INNER), (1, 2))
    edge = jnp.tile(jnp.stack([grid[0], grid[half]]) * (1.0 / INNER), (1, 2))
    return wide, edge


def product(left, right):
    return jnp.dot(left, right, preferred_element_type=jnp.float32)


def outer_stage(values, first, twist, mixed, index, count):
    half = twist.shape[1]
    sums = product(first[0], values) + product(first[1], values)
    real, imag = sums[:half], sums[half:]
    cosine, sine = twist[0], twist[1]
    turned = (real * cosine + imag * sine, imag * cosine - real * sine)
    for piece in range(2 * INNER // LANES):
        part, lane = divmod(piece * LANES, INNER)
        mixed.at[piece][pl.ds(index, half, stride=count), :] = turned[part][:, lane : lane + LANES]


def mixed_rows(mixed, start, size):
    return jnp.concatenate([mixed[piece, pl.ds(start, size), :] for piece in range(mixed.shape[0])], axis=1)


def inner_stage(values, gain, inner, back):
    rows = values.astype(jnp.bfloat16)
    spectrum = product(rows, inner[0]) + product(rows, inner[1])
    channels = gain.shape[0]
    spectrum = spectrum.reshape(channels, -1, 2 * INNER) * gain[:, None, :]
    spectrum = spectrum.reshape(-1, 2 * INNER)
    upper = spectrum.astype(jnp.bfloat16)
    lower = (spectrum - upper.astype(jnp.float32)).astype(jnp.bfloat16)
    return product(upper, back[0]) + product(lower, back[0]) + product(upper, back[1])


def edge_stage(values, gain, inner, back, turn):
    low, high = values[:, :INNER], values[:, INNER:]
    cosine, sine = turn[0:1], turn[1:2]
    rows = jnp.concatenate(
        [
            jnp.concatenate([low, jnp.zeros_like(low)], axis=1),
            jnp.concatenate([high * cosine, -high * sine], axis=1),
        ]
    )
    result = inner_stage(rows, gain, inner, back)
    size = values.shape[0]
    low = result[:size, :INNER]
    high = result[size:, :INNER] * cosine - result[size:, INNER:] * sine
    return jnp.concatenate([low, high], axis=1)


MESH = pl.DeviceIdType.MESH


def whiten_gram_kernel(
    panel_ref, first_ref, twist_ref, inner_ref, back_ref, gain_ref, edge_ref, turn_ref, out_ref,
    series, mixed, staged, landed, flat, partial, pair_land, plane_land, summed, line_land,
    send_in, recv_in, send_out, recv_out, local_sem,
    send_pair, recv_pair, send_plane, recv_plane, send_line, recv_line,
    *, tm_count, col_count, scale,
):
    my_tm, my_col = lax.axis_index("tm"), lax.axis_index("col")
    me = my_col * tm_count + my_tm
    devices = tm_count * col_count
    chunks, _, count, steps, _ = series.shape
    half = twist_ref.shape[1]
    share = half // devices

    barrier = pltpu.get_barrier_semaphore()

    @pl.loop(1, devices)
    def _(offset):
        peer = lax.rem(me + offset, devices)
        there = {"tm": lax.rem(peer, tm_count), "col": peer // tm_count}
        pl.semaphore_signal(barrier, inc=1, device_id=there, device_id_type=MESH)

    pl.semaphore_wait(barrier, devices - 1)

    def copy_in(chunk, target, sender):
        return pltpu.make_async_remote_copy(
            src_ref=panel_ref.at[target, pl.ds(chunk * count, count)],
            dst_ref=series.at[chunk, sender],
            send_sem=send_in.at[chunk, target],
            recv_sem=recv_in.at[chunk, sender],
            device_id={"tm": target, "col": my_col},
            device_id_type=MESH,
        )

    def keep_in(chunk):
        return pltpu.make_async_copy(
            panel_ref.at[my_tm, pl.ds(chunk * count, count)], series.at[chunk, my_tm], local_sem.at[0, chunk]
        )

    def copy_out(chunk, target, sender):
        return pltpu.make_async_remote_copy(
            src_ref=staged.at[chunk, pl.ds(target * share, share)],
            dst_ref=landed.at[:, sender, chunk],
            send_sem=send_out.at[chunk, target],
            recv_sem=recv_out.at[chunk, sender],
            device_id={"tm": lax.rem(target, tm_count), "col": target // tm_count},
            device_id_type=MESH,
        )

    def keep_out(chunk):
        return pltpu.make_async_copy(
            staged.at[chunk, pl.ds(me * share, share)], landed.at[:, me, chunk], local_sem.at[1, chunk]
        )

    def start_in(chunk):
        @pl.loop(1, tm_count)
        def _(offset):
            copy_in(chunk, lax.rem(my_tm + offset, tm_count), my_tm).start()

        keep_in(chunk).start()

    start_in(0)
    channels = max(share, min(half, 32))
    targets = channels // share
    tiles = half // channels

    @pl.loop(0, chunks)
    def _(chunk):
        @pl.loop(1, tm_count)
        def _(offset):
            peer = lax.rem(my_tm + offset, tm_count)
            copy_in(chunk, peer, peer).wait_recv()

        keep_in(chunk).wait()

        @pl.when(chunk + 1 < chunks)
        def _():
            start_in(chunk + 1)

        @pl.loop(0, count)
        def _(index):
            values = series[chunk, :, index].reshape(tm_count * steps, INNER)
            outer_stage(values, first_ref, twist_ref, mixed, index, count)

        @pl.loop(0, tiles)
        def _(turn):
            per_side = tiles // 2
            side = lax.rem(my_col // (col_count // 2) + 1 + turn // per_side, 2)
            shift = lax.rem(my_col, col_count // 2) * (tiles // col_count)
            tile = side * per_side + lax.rem(turn + shift, per_side)
            start = pl.multiple_of(tile * channels, channels)
            rows = mixed_rows(mixed, start * count, channels * count)
            result = inner_stage(rows, gain_ref[pl.ds(start, channels), :], inner_ref, back_ref)
            staged[chunk, pl.ds(start, channels)] = result.reshape(channels, count, 2 * INNER).astype(
                staged.dtype
            )

            @pl.when(tile == 0)
            def _():
                staged[chunk, 0] = edge_stage(
                    mixed_rows(mixed, 0, count), edge_ref[...], inner_ref, back_ref, turn_ref
                ).astype(staged.dtype)

            @pl.loop(0, targets)
            def _(place):
                target = tile * targets + lax.rem(place + my_tm, targets)

                @pl.when(target != me)
                def _():
                    copy_out(chunk, target, me).start()

                @pl.when(target == me)
                def _():
                    keep_out(chunk).start()

    col_rows, width = out_ref.shape

    @pl.loop(0, col_count)
    def _(offset):
        group = lax.rem(my_col + offset, col_count)

        @pl.loop(0, tm_count * chunks)
        def _(item):
            peer, chunk = group * tm_count + item // chunks, lax.rem(item, chunks)

            @pl.when(peer != me)
            def _():
                copy_out(chunk, peer, peer).wait_recv()

            @pl.when(peer == me)
            def _():
                keep_out(chunk).wait()

        for channel in range(share):
            flat[channel, pl.ds(pl.multiple_of(group * col_rows, col_rows), col_rows)] = landed[
                channel, pl.ds(group * tm_count, tm_count)
            ].reshape(col_rows, 2 * INNER)

    parts = col_rows // width
    chips = tm_count // PAIR
    my_chip, my_core = my_tm // PAIR, lax.rem(my_tm, PAIR)
    other_core = PAIR - 1 - my_core

    def pair_copy(row):
        return pltpu.make_async_remote_copy(
            src_ref=partial.at[row, other_core],
            dst_ref=pair_land.at[row],
            send_sem=send_pair.at[row],
            recv_sem=recv_pair.at[row],
            device_id={"tm": my_chip * PAIR + other_core, "col": my_col},
            device_id_type=MESH,
        )

    def plane_copy(row, target, sender):
        return pltpu.make_async_remote_copy(
            src_ref=partial.at[row, my_core, target],
            dst_ref=plane_land.at[row, sender],
            send_sem=send_plane.at[row, target],
            recv_sem=recv_plane.at[row, sender],
            device_id={"tm": target * PAIR + my_core, "col": my_col},
            device_id_type=MESH,
        )

    def line_copy(target, sender):
        return pltpu.make_async_remote_copy(
            src_ref=summed.at[target],
            dst_ref=line_land.at[sender],
            send_sem=send_line.at[target],
            recv_sem=recv_line.at[sender],
            device_id={"tm": my_tm, "col": target},
            device_id_type=MESH,
        )

    @pl.loop(0, col_count + 2)
    def _(step):
        @pl.when(step < col_count)
        def _():
            row = lax.rem(my_col + 1 + step, col_count)

            @pl.loop(0, col_count)
            def _(j):
                total = jnp.zeros((col_rows, col_rows), jnp.float32)
                for channel in range(share):
                    left = flat[channel, pl.ds(pl.multiple_of(row * col_rows, col_rows), col_rows)]
                    right = flat[channel, pl.ds(pl.multiple_of(j * col_rows, col_rows), col_rows)]
                    total = total + lax.dot_general(
                        left, right, (((1,), (1,)), ((), ())), preferred_element_type=jnp.float32
                    )
                total = total * scale
                for part in range(parts):
                    owner = j * parts + part
                    partial[row, lax.rem(owner, PAIR), owner // PAIR] = total[:, part * width : (part + 1) * width]

            pair_copy(row).start()

        @pl.when((step >= 1) & (step < col_count + 1))
        def _():
            row = lax.rem(my_col + step, col_count)
            pair_copy(row).wait_recv()
            partial[row, my_core] = partial[row, my_core] + pair_land[row]

            @pl.loop(1, chips)
            def _(offset):
                plane_copy(row, lax.rem(my_chip + offset, chips), my_chip).start()

        @pl.when(step >= 2)
        def _():
            row = lax.rem(my_col + step - 1, col_count)
            summed[row] = partial[row, my_core, my_chip]

            @pl.loop(1, chips)
            def _(offset):
                peer = lax.rem(my_chip + offset, chips)
                plane_copy(row, peer, peer).wait_recv()
                summed[row] = summed[row] + plane_land[row, peer]

            @pl.when(row != my_col)
            def _():
                line_copy(row, my_col).start()

    out_ref[...] = summed[my_col]

    @pl.loop(1, col_count)
    def _(offset):
        peer = lax.rem(my_col + offset, col_count)
        line_copy(peer, peer).wait_recv()
        out_ref[...] = out_ref[...] + line_land[peer]

    @pl.loop(0, col_count)
    def _(row):
        pair_copy(row).wait_send()

        @pl.loop(1, chips)
        def _(offset):
            plane_copy(row, lax.rem(my_chip + offset, chips), my_chip).wait_send()

        @pl.when(row != my_col)
        def _():
            line_copy(row, my_col).wait_send()

    @pl.loop(0, chunks)
    def _(chunk):
        @pl.loop(1, tm_count)
        def _(offset):
            copy_in(chunk, lax.rem(my_tm + offset, tm_count), my_tm).wait_send()

        @pl.loop(1, devices)
        def _(offset):
            copy_out(chunk, lax.rem(me + offset, devices), me).wait_send()


def whiten_gram(grouped, tables, gains, col_count, scale):
    first, twist, inner, back, turn = tables
    gain, edge = gains
    tm_count, per_device, steps, _ = grouped.shape
    half = twist.shape[1]
    count = math.gcd(per_device, 8)
    chunks = per_device // count
    devices = tm_count * col_count
    columns = devices * per_device
    chips = tm_count // PAIR
    block = (columns // col_count, columns // tm_count)
    vmem = pl.BlockSpec(memory_space=pltpu.VMEM)
    return pl.pallas_call(
        functools.partial(whiten_gram_kernel, tm_count=tm_count, col_count=col_count, scale=scale),
        in_specs=[pl.BlockSpec(memory_space=pl.ANY)] + [vmem] * 7,
        out_specs=vmem,
        out_shape=jax.ShapeDtypeStruct(block, jnp.float32),
        scratch_shapes=[
            pltpu.VMEM((chunks, tm_count, count, steps, INNER), jnp.bfloat16),
            pltpu.VMEM((2 * INNER // LANES, half * count, LANES), jnp.float32),
            pltpu.VMEM((chunks, half, count, 2 * INNER), jnp.bfloat16),
            pltpu.VMEM((half // devices, devices, chunks, count, 2 * INNER), jnp.bfloat16),
            pltpu.VMEM((half // devices, columns, 2 * INNER), jnp.bfloat16),
            pltpu.VMEM((col_count, PAIR, chips, *block), jnp.float32),
            pltpu.VMEM((col_count, chips, *block), jnp.float32),
            pltpu.VMEM((col_count, chips, *block), jnp.float32),
            pltpu.VMEM((col_count, *block), jnp.float32),
            pltpu.VMEM((col_count, *block), jnp.float32),
            pltpu.SemaphoreType.DMA((chunks, tm_count)),
            pltpu.SemaphoreType.DMA((chunks, tm_count)),
            pltpu.SemaphoreType.DMA((chunks, devices)),
            pltpu.SemaphoreType.DMA((chunks, devices)),
            pltpu.SemaphoreType.DMA((2, chunks)),
            pltpu.SemaphoreType.DMA((col_count,)),
            pltpu.SemaphoreType.DMA((col_count,)),
            pltpu.SemaphoreType.DMA((col_count, chips)),
            pltpu.SemaphoreType.DMA((col_count, chips)),
            pltpu.SemaphoreType.DMA((col_count,)),
            pltpu.SemaphoreType.DMA((col_count,)),
        ],
        compiler_params=pltpu.CompilerParams(
            collective_id=0, has_side_effects=True, vmem_limit_bytes=VMEM_BYTES
        ),
    )(grouped, first, twist, inner, back, gain, edge, turn)


def on_device(panel, response):
    col_rows, epoch_count = panel.shape
    tm_count = lax.axis_size("tm")
    total_len = tm_count * epoch_count
    tables = tuple(jnp.asarray(table) for table in make_tables(total_len))
    gains = gain_tables(response, total_len)
    grouped = panel.reshape(tm_count, col_rows // tm_count, epoch_count // INNER, INNER)
    col_count = lax.axis_size("col")
    return whiten_gram(grouped, tables, gains, col_count, INNER / total_len / total_len)


def solution(mesh):
    in_specs = (P("col", "tm"), P())
    out_specs = P("col", "tm")
    return jax.shard_map(
        on_device, mesh=mesh, in_specs=in_specs, out_specs=out_specs, check_vma=False
    )
```
